32 devices in a mesh: tile: 8 (over z, x), head: 4 (over y, core).
Axes of the slice: x: 2, y: 2, z: 4, core: 2. Of those that a mesh axis runs over, the one named last changes fastest.
Arguments:
- tiles: bfloat16 [3072, 768], P('tile', 'head'), may hold values from -1 to 1
- first_norm_gain: float32 [768], replicated, may hold values from 0.5 to 1.5
- query_key_value_weight: bfloat16 [768, 3, 768], P(None, None, 'head'), may hold values from -1 to 1
- attention_out_weight: bfloat16 [768, 768], P('head'), may hold values from -0.21875 to 0.21875
- second_norm_gain: float32 [768], replicated, may hold values from 0.5 to 1.5
- first_feed_weight: bfloat16 [768, 3072], P(None, 'head'), may hold values from -0.21875 to 0.21875
- second_feed_weight: bfloat16 [3072, 768], P('head'), may hold values from -0.109375 to 0.109375
- slide_tile_counts: int32 [6], replicated, may hold values from 1 to 1536, 3072 in all
- dilation_head_offsets: int32 [12], P('head'), may hold values from 0 to 3
Outputs:
- layer_out: bfloat16 [3072, 768], P('tile', 'head')
The draws below stay inside these ranges and needn't reach their ends.
Inputs may be any that keep to these rules, and one draw needn't show every extreme that they name: `slide_tile_counts`: the lengths sum to 3072; the longest is exactly 1536.
All inputs are finite; a program needn't handle non-finite values.
Results may differ from the reference program's by a relative error of at most 0.02.
Values may be sent and summed in bfloat16 or wider, within the bound.
A program may use at most 64 MiB of HBM per device.

```python
import math
import jax
import jax.numpy as jnp
import numpy as np
from jax import lax

D = 768
HEAD_COUNT = 12
HDIM = 64
FF = 3072
SLIDES = 6
TOKENS = 3072
SEG0 = 768
LEVELS = 3
N_TILE = 8
N_HEAD = 4


def draw_tiles(key, part):
    key = jax.random.fold_in(key, 11)
    amplitude = 0.03
    values = jax.random.normal(key, (TOKENS, D), jnp.float32)
    return (values * amplitude).astype(jnp.bfloat16)


def draw_query_key_value_weight(key, part):
    key = jax.random.fold_in(key, 12)
    spread = D ** (-0.5)
    weights = jax.random.normal(key, (D, 3, D), jnp.float32) * spread
    return weights.astype(jnp.bfloat16)


def touch_ends(result, key, low, largest):
    extent = result.shape
    index_at = [jax.random.randint(jax.random.fold_in(key, axis), (), 0, extent[axis]) for axis in range(len(extent))]
    result = result.at[tuple(index_at)].set(low)
    longest = extent.index(max(extent))
    index_at[longest] = (index_at[longest] + 1) % extent[longest]
    return result.at[tuple(index_at)].set(largest)


def level_of(stream_key, extent, pieces, low, largest):
    level, own = 1.0, jax.random.fold_in(stream_key, 6)
    for dim, parts in pieces:
        draws = jnp.exp(jax.random.uniform(jax.random.fold_in(own, dim), (parts,), jnp.float32, low / len(pieces), largest / len(pieces)))
        level = level * jnp.repeat(draws, extent[dim] // parts).reshape([-1 if axis == dim else 1 for axis in range(len(extent))])
    return level


def profile(count, total, reach, lean):
    portions = [(1 << 20) // math.isqrt(grade ** lean) + 1 for grade in range(2, count + 1)]
    rest, given = total - reach - (count - 1), [1] * (count - 1)
    while rest > 0:
        movable = [i for i in range(count - 1) if given[i] < reach]
        whole, remaining = sum([portions[i] for i in movable]), rest
        for i in movable:
            extra = min(reach - given[i], max(1, remaining * portions[i] // whole), rest)
            given[i] = given[i] + extra
            rest = rest - extra
    return np.array([reach] + given)


def uneven(own_key, count, total, limit, slope):
    if count == 2:
        one = jax.random.randint(own_key, (), max(1, total - limit), min(limit, total - 1) + 1)
        return jnp.stack([one, total - one])
    tallies = jnp.asarray(profile(count, total, limit, slope), jnp.int32)
    couples = (count - 1) // 2
    giver, sink = tallies[1:1 + 2 * couples:2], tallies[2:2 + 2 * couples:2]
    margin = jnp.minimum(giver - 1, limit - sink)
    shifted = jax.random.randint(jax.random.fold_in(own_key, 1), (couples,), 0, 1 << 20) % (margin + 1)
    tallies = tallies.at[1:1 + 2 * couples:2].set(giver - shifted).at[2:2 + 2 * couples:2].set(sink + shifted)
    return tallies[jax.random.permutation(jax.random.fold_in(own_key, 2), count)]


def gaussian(own_key, extent, deviation, most, shards=(), kind=jnp.bfloat16):
    result = jax.random.normal(own_key, extent, jnp.float32) * deviation
    if len(shards) > 0:
        result = level_of(own_key, extent, shards, -0.22, 0.18) * result
    return jnp.clip(result, min=-most, max=most).astype(kind)


def setup_inputs(seed: int = 0) -> dict:
    key_of = jax.random.split(jax.random.key(seed), 10)
    return {
        "tiles": draw_tiles(jax.random.fold_in(key_of[9], 71), 0),
        "first_norm_gain": jnp.clip(1.0 + 0.1 * jax.random.normal(key_of[1], (D,), jnp.float32), 0.5, 1.5),
        "query_key_value_weight": draw_query_key_value_weight(jax.random.fold_in(key_of[9], 71), 0),
        "attention_out_weight": gaussian(key_of[3], (D, D), D ** -0.5, 0.21875, ((0, 4),)),
        "second_norm_gain": jnp.clip(1.0 + 0.1 * jax.random.normal(key_of[4], (D,), jnp.float32), 0.5, 1.5),
        "first_feed_weight": gaussian(key_of[5], (D, FF), D ** -0.5, 0.21875, ((1, 4),)),
        "second_feed_weight": gaussian(key_of[6], (FF, D), FF ** -0.5, 0.109375, ((0, 4),)),
        "slide_tile_counts": uneven(key_of[7], SLIDES, TOKENS, TOKENS // 2, 2).astype(jnp.int32),
        "dilation_head_offsets": touch_ends(jax.random.randint(key_of[8], (HEAD_COUNT,), 0, N_TILE // 2), jax.random.fold_in(key_of[8], 1), 0, (N_TILE // 2) - 1).astype(jnp.int32),
    }


def layer_norm(values, gain):
    center = lax.optimization_barrier(jnp.mean(values, axis=-1, keepdims=True))
    square = lax.optimization_barrier(jnp.mean(values * values, axis=-1, keepdims=True))
    return (values - center) * lax.rsqrt(square - center * center + 1e-05) * gain

def spread_rows(values, stride_len, fill):
    count = values.shape[0]
    if values.ndim == 1:
        return jnp.broadcast_to(values[:, None], (count, stride_len)).reshape(count * stride_len)
    return jnp.broadcast_to(values[:, None, :], (count, stride_len, values.shape[1])).reshape(count * stride_len, values.shape[1])

def reference(tiles, first_norm_gain, query_key_value_weight, attention_out_weight, second_norm_gain, first_feed_weight, second_feed_weight, slide_tile_counts, dilation_head_offsets):
    slide_ends = jnp.cumsum(slide_tile_counts)[:-1].astype(jnp.int32)
    embed = tiles.astype(jnp.float32)
    ln1 = layer_norm(embed, first_norm_gain).astype(jnp.bfloat16)
    projected = [jnp.dot(ln1, query_key_value_weight[:, which, :], preferred_element_type=jnp.float32).astype(jnp.bfloat16) for which in range(3)]
    head_width = [item.reshape(TOKENS, HEAD_COUNT, HDIM).transpose(1, 0, 2) for item in projected]
    all_pos = jnp.arange(TOKENS, dtype=jnp.int32)

    def attend_single_head(inputs):
        query_h, key_h, value_h, offset = inputs
        best = None
        denom = None
        accum = None
        for level_idx in range(LEVELS):
            stride_len = 2 ** level_idx
            sel_count = TOKENS // stride_len
            seg_count = sel_count // SEG0
            phase_off = (offset % stride_len).astype(jnp.int32)
            picks = [lax.dynamic_index_in_dim(item.reshape(sel_count, stride_len, HDIM), phase_off, 1, keepdims=False) for item in (query_h, key_h, value_h)]
            positions = phase_off + stride_len * jnp.arange(sel_count, dtype=jnp.int32)
            slide_num = lax.optimization_barrier(jnp.sum((positions[:, None] >= slide_ends[None, :]).astype(jnp.int32), axis=1))

            def segment_attend(seg_in):
                seg_q, seg_k, seg_v, seg_slide = seg_in
                scores = jnp.dot(seg_q, seg_k.T, preferred_element_type=jnp.float32) * HDIM ** (-0.5)
                scores = jnp.where(seg_slide[:, None] == seg_slide[None, :], scores, jnp.float32(-1e+30))
                top_score = lax.optimization_barrier(jnp.max(scores, axis=1))
                expo = jnp.exp(scores - top_score[:, None])
                sums = lax.optimization_barrier(jnp.sum(expo, axis=1))
                weighted = jnp.dot(expo.astype(jnp.bfloat16), seg_v, preferred_element_type=jnp.float32)
                return (top_score, sums, weighted)
            top_score, sums, weighted = lax.map(segment_attend, (picks[0].reshape(seg_count, SEG0, HDIM), picks[1].reshape(seg_count, SEG0, HDIM), picks[2].reshape(seg_count, SEG0, HDIM), slide_num.reshape(seg_count, SEG0)))
            picked = all_pos % stride_len == phase_off
            top_full = jnp.where(picked, spread_rows(top_score.reshape(sel_count), stride_len, 0), jnp.float32(-1e+30))
            sum_full = jnp.where(picked, spread_rows(sums.reshape(sel_count), stride_len, 0), jnp.float32(0.0))
            acc_full = jnp.where(picked[:, None], spread_rows(weighted.reshape(sel_count, HDIM), stride_len, 0), jnp.float32(0.0))
            if level_idx == 0:
                best, denom, accum = (top_full, sum_full, acc_full)
            else:
                newest = jnp.maximum(best, top_full)
                old_weight = jnp.exp(best - newest)
                new_weight = jnp.exp(top_full - newest)
                denom = denom * old_weight + sum_full * new_weight
                accum = accum * old_weight[:, None] + acc_full * new_weight[:, None]
                best = newest
        return accum / denom[:, None]
    attended_rows = lax.map(attend_single_head, (head_width[0], head_width[1], head_width[2], dilation_head_offsets))
    attn = attended_rows.astype(jnp.bfloat16).transpose(1, 0, 2).reshape(TOKENS, D)
    group_feat = D // N_HEAD
    attn_out = jnp.zeros((TOKENS, D), jnp.float32)
    for group in range(N_HEAD):
        term = jnp.dot(attn[:, group * group_feat:(group + 1) * group_feat], attention_out_weight[group * group_feat:(group + 1) * group_feat], preferred_element_type=jnp.float32).astype(jnp.bfloat16)
        attn_out = attn_out + lax.optimization_barrier(term).astype(jnp.float32)
    resid = (embed + attn_out).astype(jnp.bfloat16)
    ln2 = layer_norm(resid.astype(jnp.float32), second_norm_gain).astype(jnp.bfloat16)
    hidden = jax.nn.gelu(jnp.dot(ln2, first_feed_weight, preferred_element_type=jnp.float32)).astype(jnp.bfloat16)
    group_hid = FF // N_HEAD
    mlp_out = jnp.zeros((TOKENS, D), jnp.float32)
    for group in range(N_HEAD):
        term = jnp.dot(hidden[:, group * group_hid:(group + 1) * group_hid], second_feed_weight[group * group_hid:(group + 1) * group_hid], preferred_element_type=jnp.float32).astype(jnp.bfloat16)
        mlp_out = mlp_out + lax.optimization_barrier(term).astype(jnp.float32)
    return (resid.astype(jnp.float32) + mlp_out).astype(jnp.bfloat16)
```

```python
import functools

import jax
import jax.numpy as jnp
from jax import lax
from jax.experimental import pallas as pl
from jax.experimental.pallas import tpu as pltpu
from jax.sharding import PartitionSpec as P

HDIM = 64
WIDE = 2 * HDIM
CHUNK = 128
MASKED = -1e30
F32 = jnp.float32
BF16 = jnp.bfloat16


def dot(left, right):
    return jnp.dot(left, right, preferred_element_type=F32)


def padded_rows(rows, level):
    return -(-(rows >> level) // 16) * 16


def key_layout(rows, tile_count):
    pieces, start = {}, rows
    for m in range(1, tile_count):
        level = m.bit_length() - 1
        count = padded_rows(rows, level)
        pieces[m] = (level, start, count)
        start += count
    return pieces, start


def layer_norm_blocks(blocks, gains, width):
    total = sum(jnp.sum(b, axis=-1, keepdims=True) for b in blocks)
    squares = sum(jnp.sum(b * b, axis=-1, keepdims=True) for b in blocks)
    center = total / width
    scale = lax.rsqrt(squares / width - center * center + 1e-05)
    return [((b - center) * scale * g).astype(BF16) for b, g in zip(blocks, gains)]


def kernel(
    tile_count,
    group_count,
    slide_count,
    tiles_ref,
    gain1_ref,
    qkv_hbm,
    wo_hbm,
    gain2_ref,
    w1_hbm,
    w2_hbm,
    counts_ref,
    offsets_ref,
    out_ref,
    wqkv,
    wo,
    w1,
    w2,
    wo_split,
    w2_split,
    xfull,
    rfull,
    qaug,
    kvbuf,
    select_buf,
    top_buf,
    acc_buf,
    attn_buf,
    keep_buf,
    side_send,
    side_recv,
    far_send,
    far_recv,
    load_sem,
    send_sem,
    recv_sem,
):
    rows, share = tiles_ref.shape
    heads = offsets_ref.shape[0]
    levels = tile_count.bit_length() - 1
    chunks = rows // CHUNK
    width = share * group_count
    pieces, key_rows = key_layout(rows, tile_count)
    t = lax.axis_index("tile")
    h = lax.axis_index("head")
    sib, far, diag = h ^ 1, h ^ 2, h ^ 3

    loads = [
        pltpu.make_async_copy(src, dst, load_sem.at[i])
        for i, (src, dst) in enumerate(((qkv_hbm, wqkv), (wo_hbm, wo), (w1_hbm, w1), (w2_hbm, w2)))
    ]
    for load in loads:
        load.start()

    barrier = pltpu.get_barrier_semaphore()
    for peer in (sib, far):
        pl.semaphore_signal(
            barrier, inc=1, device_id=(t, peer), device_id_type=pl.DeviceIdType.MESH
        )
    for m in range(1, tile_count):
        pl.semaphore_signal(
            barrier, inc=1, device_id=(t ^ m, h), device_id_type=pl.DeviceIdType.MESH
        )
    pl.semaphore_wait(barrier, tile_count + 1)

    used = [0]
    sent = []

    def send(src, dst, tile, head):
        index = used[0]
        used[0] += 1
        copy = pltpu.make_async_remote_copy(
            src_ref=src,
            dst_ref=dst,
            send_sem=send_sem.at[index],
            recv_sem=recv_sem.at[index],
            device_id=(tile, head),
            device_id_type=pl.DeviceIdType.MESH,
        )
        copy.start()
        sent.append(copy)
        return copy

    def span(c):
        return pl.ds(c * CHUNK, CHUNK)

    own_far, own_side = [], []
    for c in range(chunks):
        own_far.append(send(tiles_ref.at[span(c)], xfull.at[h, span(c)], t, far))
        own_side.append(send(tiles_ref.at[span(c)], xfull.at[h, span(c)], t, sib))

    lane_row = lax.broadcasted_iota(jnp.int32, (1, WIDE), 1)
    low = jnp.full((1, WIDE), -1, jnp.int32)
    high = jnp.full((1, WIDE), 1 << 30, jnp.int32)
    total = jnp.int32(0)
    for j in range(slide_count - 1):
        total = total + counts_ref[j]
        high = jnp.where(lane_row == HDIM + j, total, high)
        low = jnp.where(lane_row == HDIM + j + 1, total, low)
    is_slide = (lane_row >= HDIM) & (lane_row < HDIM + slide_count)

    def row_iota(count):
        return lax.broadcasted_iota(jnp.int32, (count, WIDE), 0)

    def lane_iota(count):
        return lax.broadcasted_iota(jnp.int32, (count, WIDE), 1)

    offs = [offsets_ref[i] for i in range(heads)]

    def query_features(i):
        posn = t * rows + row_iota(rows)
        lane = lane_iota(rows)
        inside = (posn >= low) & (posn < high) & is_slide
        feats = jnp.where(inside, F32(1), F32(0))
        for level in range(1, levels):
            step = 1 << level
            other = (posn & (step - 1)) != (offs[i] & (step - 1))
            feats = jnp.where((lane == HDIM + slide_count + level - 1) & other, F32(1), feats)
        return feats

    for i in range(heads):
        qaug[i] = query_features(i).astype(BF16)

    for load in loads[:2]:
        load.wait()
    for b in range(group_count):
        wo_split[b] = wo[:, b * share : (b + 1) * share]
    for load in loads[2:]:
        load.wait()
    for b in range(group_count):
        w2_split[b] = w2[:, b * share : (b + 1) * share]

    def project(c, passed):
        own_side[c].wait_recv()
        passed.wait_recv()
        blocks = [
            jnp.where(
                h == b, tiles_ref[span(c)].astype(F32), xfull[b, span(c)].astype(F32)
            )
            for b in range(group_count)
        ]
        normed = layer_norm_blocks(blocks, [gain1_ref[b : b + 1] for b in range(group_count)], width)
        parts = []
        for kind in range(3):
            acc = None
            for b in range(group_count):
                term = dot(normed[b], wqkv[kind, b * share : (b + 1) * share, :])
                acc = term if acc is None else acc + term
            parts.append(acc)
        query, key, value = parts
        query = query.astype(BF16).astype(F32) * F32(HDIM ** (-0.5))
        for i in range(heads):
            own = slice(i * HDIM, (i + 1) * HDIM)
            qaug[i, span(c), 0:HDIM] = query[:, own].astype(BF16)
            kvbuf[i, span(c), 0:HDIM] = key[:, own].astype(BF16)
            kvbuf[i, span(c), HDIM:WIDE] = value[:, own].astype(BF16)

    passed = []
    for c in range(chunks):
        own_far[c].wait_recv()
        passed.append(send(xfull.at[far, span(c)], xfull.at[far, span(c)], t, sib))
        if c > 0:
            project(c - 1, passed[c - 1])
    project(chunks - 1, passed[chunks - 1])

    key_copy = {}

    def send_piece(m):
        level, start, count = pieces[m]
        if level == 0:
            src = kvbuf.at[:, pl.ds(0, count)]
        else:
            src = select_buf.at[:, pl.ds(select_start[level], count)]
        key_copy[m] = send(src, kvbuf.at[:, pl.ds(start, count)], t ^ m, h)

    select_start, at = {}, 0
    for level in range(1, levels):
        select_start[level] = at
        at += padded_rows(rows, level)
    send_piece(1)
    for level in range(levels - 1, 0, -1):
        count = padded_rows(rows, level)
        step = 1 << level
        want = lax.broadcasted_iota(jnp.int32, (count, rows), 0) * step
        have = lax.broadcasted_iota(jnp.int32, (count, rows), 1)
        for i in range(heads):
            pick = jnp.where(have == want + (offs[i] & (step - 1)), F32(1), F32(0)).astype(BF16)
            select_buf[i, pl.ds(select_start[level], count), :] = dot(
                pick, kvbuf[i, pl.ds(0, rows), :]
            ).astype(BF16)
        for m in range(1 << level, 2 << level):
            send_piece(m)

    def attend(i, members, level, first):
        off = offs[i]
        step = 1 << level
        augs, posns, keys = [], [], []
        for m in members:
            if m == 0:
                start, count = 0, rows
            else:
                _, start, count = pieces[m]
            local = row_iota(count) * step + (off & (step - 1))
            posn = (t ^ m) * rows + local
            both = kvbuf[i, pl.ds(start, count), :].astype(F32)
            inside = (posn >= low) & (posn < high) & (local < rows)
            feats = jnp.where(is_slide & jnp.logical_not(inside), F32(MASKED), F32(0))
            if level > 0:
                feats = jnp.where(
                    lane_iota(count) == HDIM + slide_count + level - 1, F32(MASKED), feats
                )
            augs.append(jnp.where(lane_iota(count) < HDIM, both, feats).astype(BF16))
            keys.append(both)
            posns.append(posn)
        aug = augs[0] if len(augs) == 1 else jnp.concatenate(augs, axis=0)
        both = keys[0] if len(keys) == 1 else jnp.concatenate(keys, axis=0)
        posn = posns[0] if len(posns) == 1 else jnp.concatenate(posns, axis=0)
        scores = lax.dot_general(
            qaug[i], aug, (((1,), (1,)), ((), ())), preferred_element_type=F32
        )
        top = jnp.max(scores, axis=1, keepdims=True)
        if not first:
            before = top_buf[i][:, 0:1]
            top = jnp.maximum(top, before)
        expo = jnp.exp(scores - top).astype(BF16)
        summed = jnp.where(lane_iota(both.shape[0]) < HDIM, F32(1), both)
        acc = None
        query_posn = t * rows + row_iota(rows)
        for l in range(level, levels):
            mod = (1 << l) - 1
            weights = summed
            if l > level:
                weights = jnp.where((posn & mod) == (off & mod), summed, F32(0))
            term = dot(expo, weights.astype(BF16))
            if l > 0:
                term = jnp.where((query_posn & mod) == (off & mod), term, F32(0))
            acc = term if acc is None else acc + term
        if not first:
            acc = acc + acc_buf[i] * jnp.exp(before - top)
        acc_buf[i] = acc
        top_buf[i] = jnp.broadcast_to(top, (rows, WIDE))

    for i in range(heads):
        attend(i, [0], 0, True)
    for level in range(levels):
        members = list(range(1 << level, 2 << level))
        for m in members:
            key_copy[m].wait_recv()
        for i in range(heads):
            attend(i, members, level, False)
    for i in range(heads):
        acc = acc_buf[i]
        attn_buf[i] = (acc[:, HDIM:WIDE] / acc[:, 0:1]).astype(BF16)

    side1, far1, side2, far2 = {}, {}, {}, {}
    res_far, res_side, res_pass = {}, {}, {}

    def spread_terms(which, c, block):
        for j, to in enumerate((sib, diag)):
            side_send[which, c, j] = block(to).astype(BF16)
        copy = send(side_send.at[which, c], side_recv.at[which, c], t, sib)
        for j, to in enumerate((far, h)):
            keep_buf[which, c, j] = block(to)
        return copy

    def cross(which, c, side):
        side.wait_recv()
        far_send[which, c] = (
            keep_buf[which, c, 0].astype(BF16).astype(F32) + side_recv[which, c, 1].astype(F32)
        ).astype(BF16)
        return send(far_send.at[which, c], far_recv.at[which, c], t, far)

    def gathered(which, c):
        return (
            keep_buf[which, c, 1].astype(BF16).astype(F32)
            + side_recv[which, c, 0].astype(F32)
            + far_recv[which, c].astype(F32)
        )

    def stage_out(c):
        def block(to):
            acc = None
            for i in range(heads):
                term = dot(attn_buf[i, span(c), :], wo_split[to, i * HDIM : (i + 1) * HDIM, :])
                acc = term if acc is None else acc + term
            return acc

        side1[c] = spread_terms(0, c, block)

    def stage_cross1(c):
        far1[c] = cross(0, c, side1[c])

    def stage_resid(c):
        far1[c].wait_recv()
        rfull[h, span(c)] = (tiles_ref[span(c)].astype(F32) + gathered(0, c)).astype(BF16)
        res_far[c] = send(rfull.at[h, span(c)], rfull.at[h, span(c)], t, far)
        res_side[c] = send(rfull.at[h, span(c)], rfull.at[h, span(c)], t, sib)

    def stage_pass(c):
        res_far[c].wait_recv()
        res_pass[c] = send(rfull.at[far, span(c)], rfull.at[far, span(c)], t, sib)

    def stage_feed(c):
        res_side[c].wait_recv()
        res_pass[c].wait_recv()
        blocks = [rfull[b, span(c)].astype(F32) for b in range(group_count)]
        normed = layer_norm_blocks(blocks, [gain2_ref[b : b + 1] for b in range(group_count)], width)
        acc = None
        for b in range(group_count):
            term = dot(normed[b], w1[b * share : (b + 1) * share, :])
            acc = term if acc is None else acc + term
        hidden = jax.nn.gelu(acc).astype(BF16)
        side2[c] = spread_terms(1, c, lambda to: dot(hidden, w2_split[to]))

    def stage_cross2(c):
        far2[c] = cross(1, c, side2[c])

    def stage_last(c):
        far2[c].wait_recv()
        out_ref[span(c)] = (rfull[h, span(c)].astype(F32) + gathered(1, c)).astype(BF16)

    stages = [
        stage_out,
        stage_cross1,
        stage_resid,
        stage_pass,
        stage_feed,
        stage_cross2,
        stage_last,
    ]
    for step in range(chunks + len(stages) - 1):
        for place in range(len(stages) - 1, -1, -1):
            c = step - place
            if 0 <= c < chunks:
                stages[place](c)
    for copy in sent:
        copy.wait_send()


def local(
    tile_count,
    group_count,
    tiles,
    first_norm_gain,
    query_key_value_weight,
    attention_out_weight,
    second_norm_gain,
    first_feed_weight,
    second_feed_weight,
    slide_tile_counts,
    dilation_head_offsets,
):
    rows, share = tiles.shape
    heads = dilation_head_offsets.shape[0]
    levels = tile_count.bit_length() - 1
    chunks = rows // CHUNK
    _, key_rows = key_layout(rows, tile_count)
    select_rows = max(16, sum(padded_rows(rows, level) for level in range(1, levels)))
    copies = 10 * chunks + tile_count - 1
    vmem = pl.BlockSpec(memory_space=pltpu.VMEM)
    smem = pl.BlockSpec(memory_space=pltpu.SMEM)
    anywhere = pl.BlockSpec(memory_space=pl.ANY)
    hidden = first_feed_weight.shape[1]
    width = share * group_count
    return pl.pallas_call(
        functools.partial(kernel, tile_count, group_count, slide_tile_counts.shape[0]),
        out_shape=jax.ShapeDtypeStruct((rows, share), BF16),
        in_specs=[vmem, vmem, anywhere, anywhere, vmem, anywhere, anywhere, smem, smem],
        out_specs=vmem,
        scratch_shapes=[
            pltpu.VMEM((3, width, share), BF16),
            pltpu.VMEM((share, width), BF16),
            pltpu.VMEM((width, hidden), BF16),
            pltpu.VMEM((hidden, width), BF16),
            pltpu.VMEM((group_count, share, share), BF16),
            pltpu.VMEM((group_count, hidden, share), BF16),
            pltpu.VMEM((group_count, rows, share), BF16),
            pltpu.VMEM((group_count, rows, share), BF16),
            pltpu.VMEM((heads, rows, WIDE), BF16),
            pltpu.VMEM((heads, key_rows, WIDE), BF16),
            pltpu.VMEM((heads, select_rows, WIDE), BF16),
            pltpu.VMEM((heads, rows, WIDE), F32),
            pltpu.VMEM((heads, rows, WIDE), F32),
            pltpu.VMEM((heads, rows, HDIM), BF16),
            pltpu.VMEM((2, chunks, 2, CHUNK, share), F32),
            pltpu.VMEM((2, chunks, 2, CHUNK, share), BF16),
            pltpu.VMEM((2, chunks, 2, CHUNK, share), BF16),
            pltpu.VMEM((2, chunks, CHUNK, share), BF16),
            pltpu.VMEM((2, chunks, CHUNK, share), BF16),
            pltpu.SemaphoreType.DMA((4,)),
            pltpu.SemaphoreType.DMA((copies,)),
            pltpu.SemaphoreType.DMA((copies,)),
        ],
        compiler_params=pltpu.CompilerParams(
            collective_id=0, has_side_effects=True, vmem_limit_bytes=48 << 20
        ),
    )(
        tiles,
        first_norm_gain.reshape(group_count, share),
        jnp.transpose(query_key_value_weight, (1, 0, 2)),
        attention_out_weight,
        second_norm_gain.reshape(group_count, share),
        first_feed_weight,
        second_feed_weight,
        slide_tile_counts,
        dilation_head_offsets,
    )


def solution(mesh):
    return jax.shard_map(
        functools.partial(local, mesh.shape["tile"], mesh.shape["head"]),
        mesh=mesh,
        in_specs=(
            P("tile", "head"),
            P(),
            P(None, None, "head"),
            P("head", None),
            P(),
            P(None, "head"),
            P("head", None),
            P(),
            P("head"),
        ),
        out_specs=P("tile", "head"),
        check_vma=False,
    )
```

```python
import functools

import jax
import jax.numpy as jnp
from jax import lax
from jax.experimental import pallas as pl
from jax.experimental.pallas import tpu as pltpu
from jax.sharding import PartitionSpec as P

HDIM = 64
WIDE = 2 * HDIM
CHUNK = 128
MASKED = -1e30
F32 = jnp.float32
BF16 = jnp.bfloat16


def dot(left, right):
    return jnp.dot(left, right, preferred_element_type=F32)


def padded_rows(rows, level):
    return -(-(rows >> level) // 16) * 16


def key_layout(rows, tile_count):
    pieces, start = {}, rows
    for m in range(1, tile_count):
        level = m.bit_length() - 1
        count = padded_rows(rows, level)
        pieces[m] = (level, start, count)
        start += count
    return pieces, start


def layer_norm_columns(values, gain):
    width = values.shape[0]
    center = jnp.sum(values, axis=0, keepdims=True) / width
    square = jnp.sum(values * values, axis=0, keepdims=True) / width
    scale = lax.rsqrt(square - center * center + 1e-05)
    return ((values - center) * scale * gain).astype(BF16)


def kernel(
    tile_count,
    group_count,
    slide_count,
    tiles_hbm,
    gain1_hbm,
    qkv_hbm,
    wo_hbm,
    gain2_hbm,
    w1_hbm,
    w2_hbm,
    counts_hbm,
    offsets_hbm,
    out_ref,
    tiles_ref,
    gain1_row,
    gain2_row,
    gain1,
    gain2,
    counts_ref,
    offsets_ref,
    wqkv,
    wo,
    w1,
    w2,
    wo_turned,
    w1_turned,
    w2_turned,
    xfull,
    rfull,
    qaug,
    kvbuf,
    select_buf,
    top_buf,
    acc_buf,
    attn_buf,
    keep_buf,
    side_send,
    side_recv,
    far_send,
    far_recv,
    load_sem,
    send_sem,
    recv_sem,
):
    share, rows = tiles_ref.shape
    heads = offsets_ref.shape[0]
    levels = tile_count.bit_length() - 1
    chunks = rows // CHUNK
    width = share * group_count
    pieces, key_rows = key_layout(rows, tile_count)
    t = lax.axis_index("tile")
    h = lax.axis_index("head")
    sib, far, diag = h ^ 1, h ^ 2, h ^ 3

    loads = [
        pltpu.make_async_copy(src, dst, load_sem.at[i])
        for i, (src, dst) in enumerate(
            (
                (tiles_hbm, tiles_ref),
                (counts_hbm, counts_ref),
                (offsets_hbm, offsets_ref),
                (gain1_hbm, gain1_row),
                (gain2_hbm, gain2_row),
                (wo_hbm, wo),
                (w1_hbm, w1),
                (w2_hbm, w2),
                (qkv_hbm, wqkv),
            )
        )
    ]
    for load in loads:
        load.start()

    barrier = pltpu.get_barrier_semaphore()
    for peer in (sib, far):
        pl.semaphore_signal(
            barrier, inc=1, device_id=(t, peer), device_id_type=pl.DeviceIdType.MESH
        )
    for m in range(1, tile_count):
        pl.semaphore_signal(
            barrier, inc=1, device_id=(t ^ m, h), device_id_type=pl.DeviceIdType.MESH
        )
    pl.semaphore_wait(barrier, tile_count + 1)

    used = [0]
    sent = []

    def send(src, dst, tile, head):
        index = used[0]
        used[0] += 1
        copy = pltpu.make_async_remote_copy(
            src_ref=src,
            dst_ref=dst,
            send_sem=send_sem.at[index],
            recv_sem=recv_sem.at[index],
            device_id=(tile, head),
            device_id_type=pl.DeviceIdType.MESH,
        )
        copy.start()
        sent.append(copy)
        return copy

    def span(c):
        return pl.ds(c * CHUNK, CHUNK)

    loads[0].wait()
    own_far, own_side = [], []
    for c in range(chunks):
        own_far.append(send(tiles_ref.at[:, span(c)], xfull.at[c, h], t, far))
    for c in range(chunks):
        own_side.append(send(tiles_ref.at[:, span(c)], xfull.at[c, h], t, sib))
    loads[1].wait()
    loads[2].wait()

    lane_row = lax.broadcasted_iota(jnp.int32, (1, WIDE), 1)
    low = jnp.full((1, WIDE), -1, jnp.int32)
    high = jnp.full((1, WIDE), 1 << 30, jnp.int32)
    total = jnp.int32(0)
    for j in range(slide_count - 1):
        total = total + counts_ref[j]
        high = jnp.where(lane_row == HDIM + j, total, high)
        low = jnp.where(lane_row == HDIM + j + 1, total, low)
    is_slide = (lane_row >= HDIM) & (lane_row < HDIM + slide_count)

    def row_iota(count):
        return lax.broadcasted_iota(jnp.int32, (count, WIDE), 0)

    def lane_iota(count):
        return lax.broadcasted_iota(jnp.int32, (count, WIDE), 1)

    offs = [offsets_ref[i] for i in range(heads)]

    def query_features(i):
        posn = t * rows + row_iota(rows)
        lane = lane_iota(rows)
        inside = (posn >= low) & (posn < high) & is_slide
        feats = jnp.where(inside, F32(1), F32(0))
        for level in range(1, levels):
            step = 1 << level
            other = (posn & (step - 1)) != (offs[i] & (step - 1))
            feats = jnp.where((lane == HDIM + slide_count + level - 1) & other, F32(1), feats)
        return feats

    for i in range(heads):
        qaug[i] = query_features(i).astype(BF16)

    for load in loads[3:]:
        load.wait()
    gain1[...] = jnp.broadcast_to(gain1_row[...][None], (CHUNK, width)).T
    gain2[...] = jnp.broadcast_to(gain2_row[...][None], (CHUNK, width)).T
    turned = wo[...].T
    for b in range(group_count):
        wo_turned[b] = turned[b * share : (b + 1) * share]
    w1_turned[...] = w1[...].T
    turned = w2[...].T
    for b in range(group_count):
        w2_turned[b] = turned[b * share : (b + 1) * share]

    def columns(blocks):
        return jnp.concatenate(blocks, axis=0).astype(F32)

    def project(c, passed):
        own_side[c].wait_recv()
        passed.wait_recv()
        own = tiles_ref[:, span(c)]
        blocks = [jnp.where(h == b, own, xfull[c, b]) for b in range(group_count)]
        normed = layer_norm_columns(columns(blocks), gain1[...])
        query, key, value = [dot(wqkv[kind], normed) for kind in range(3)]
        query = query.astype(BF16).astype(F32) * F32(HDIM ** (-0.5))
        for i in range(heads):
            own = slice(i * HDIM, (i + 1) * HDIM)
            features = jnp.concatenate([query[own], query[own]], axis=0).T
            first = lane_iota(CHUNK) < HDIM
            qaug[i, span(c), :] = jnp.where(
                first, features, qaug[i, span(c), :].astype(F32)
            ).astype(BF16)
            kvbuf[i, span(c), :] = jnp.concatenate([key[own], value[own]], axis=0).T.astype(BF16)

    passed = []
    for c in range(chunks):
        own_far[c].wait_recv()
        passed.append(send(xfull.at[c, far], xfull.at[c, far], t, sib))
    for c in range(chunks):
        project(c, passed[c])

    key_copy = {}

    def send_piece(m):
        level, start, count = pieces[m]
        if level == 0:
            src = kvbuf.at[:, pl.ds(0, count)]
        else:
            src = select_buf.at[:, pl.ds(select_start[level], count)]
        key_copy[m] = send(src, kvbuf.at[:, pl.ds(start, count)], t ^ m, h)

    select_start, at = {}, 0
    for level in range(1, levels):
        select_start[level] = at
        at += padded_rows(rows, level)
    send_piece(1)
    for level in range(levels - 1, 0, -1):
        count = padded_rows(rows, level)
        step = 1 << level
        want = lax.broadcasted_iota(jnp.int32, (count, rows), 0) * step
        have = lax.broadcasted_iota(jnp.int32, (count, rows), 1)
        for i in range(heads):
            pick = jnp.where(have == want + (offs[i] & (step - 1)), F32(1), F32(0)).astype(BF16)
            select_buf[i, pl.ds(select_start[level], count), :] = dot(
                pick, kvbuf[i, pl.ds(0, rows), :]
            ).astype(BF16)
        for m in range(1 << level, 2 << level):
            send_piece(m)

    def attend(i, members, level, first):
        off = offs[i]
        step = 1 << level
        augs, posns, keys = [], [], []
        for m in members:
            if m == 0:
                start, count = 0, rows
            else:
                _, start, count = pieces[m]
            local = row_iota(count) * step + (off & (step - 1))
            posn = (t ^ m) * rows + local
            both = kvbuf[i, pl.ds(start, count), :].astype(F32)
            inside = (posn >= low) & (posn < high) & (local < rows)
            feats = jnp.where(is_slide & jnp.logical_not(inside), F32(MASKED), F32(0))
            if level > 0:
                feats = jnp.where(
                    lane_iota(count) == HDIM + slide_count + level - 1, F32(MASKED), feats
                )
            augs.append(jnp.where(lane_iota(count) < HDIM, both, feats).astype(BF16))
            keys.append(both)
            posns.append(posn)
        aug = augs[0] if len(augs) == 1 else jnp.concatenate(augs, axis=0)
        both = keys[0] if len(keys) == 1 else jnp.concatenate(keys, axis=0)
        posn = posns[0] if len(posns) == 1 else jnp.concatenate(posns, axis=0)
        scores = lax.dot_general(
            qaug[i], aug, (((1,), (1,)), ((), ())), preferred_element_type=F32
        )
        top = jnp.max(scores, axis=1, keepdims=True)
        if not first:
            before = top_buf[i][:, 0:1]
            top = jnp.maximum(top, before)
        expo = jnp.exp(scores - top).astype(BF16)
        summed = jnp.where(lane_iota(both.shape[0]) < HDIM, F32(1), both)
        acc = None
        query_posn = t * rows + row_iota(rows)
        for l in range(level, levels):
            mod = (1 << l) - 1
            weights = summed
            if l > level:
                weights = jnp.where((posn & mod) == (off & mod), summed, F32(0))
            term = dot(expo, weights.astype(BF16))
            if l > 0:
                term = jnp.where((query_posn & mod) == (off & mod), term, F32(0))
            acc = term if acc is None else acc + term
        if not first:
            acc = acc + acc_buf[i] * jnp.exp(before - top)
        acc_buf[i] = acc
        top_buf[i] = jnp.broadcast_to(top, (rows, WIDE))

    for i in range(heads):
        attend(i, [0], 0, True)
    for level in range(levels):
        members = list(range(1 << level, 2 << level))
        for m in members:
            key_copy[m].wait_recv()
        for i in range(heads):
            attend(i, members, level, False)
    for i in range(heads):
        acc = acc_buf[i].T
        attn_buf[i * HDIM : (i + 1) * HDIM] = (acc[HDIM:WIDE] / acc[0:1]).astype(BF16)

    side1, far1, side2, far2 = {}, {}, {}, {}
    res_far, res_side, res_pass = {}, {}, {}

    def spread_terms(which, c, block):
        for j, to in enumerate((sib, diag)):
            side_send[which, c, j] = block(to).astype(BF16)
        copy = send(side_send.at[which, c], side_recv.at[which, c], t, sib)
        for j, to in enumerate((far, h)):
            keep_buf[which, c, j] = block(to)
        return copy

    def cross(which, c, side):
        side.wait_recv()
        far_send[which, c] = (
            keep_buf[which, c, 0].astype(BF16).astype(F32) + side_recv[which, c, 1].astype(F32)
        ).astype(BF16)
        return send(far_send.at[which, c], far_recv.at[which, c], t, far)

    def gathered(which, c):
        return (
            keep_buf[which, c, 1].astype(BF16).astype(F32)
            + side_recv[which, c, 0].astype(F32)
            + far_recv[which, c].astype(F32)
        )

    def stage_out(c):
        attn = attn_buf[:, span(c)]
        side1[c] = spread_terms(0, c, lambda to: dot(wo_turned[to], attn))

    def stage_cross1(c):
        far1[c] = cross(0, c, side1[c])

    def stage_resid(c):
        far1[c].wait_recv()
        rfull[c, h] = (tiles_ref[:, span(c)].astype(F32) + gathered(0, c)).astype(BF16)
        res_far[c] = send(rfull.at[c, h], rfull.at[c, h], t, far)
        res_side[c] = send(rfull.at[c, h], rfull.at[c, h], t, sib)

    def stage_pass(c):
        res_far[c].wait_recv()
        res_pass[c] = send(rfull.at[c, far], rfull.at[c, far], t, sib)

    def stage_feed(c):
        res_side[c].wait_recv()
        res_pass[c].wait_recv()
        blocks = [rfull[c, b] for b in range(group_count)]
        normed = layer_norm_columns(columns(blocks), gain2[...])
        hidden = jax.nn.gelu(dot(w1_turned[...], normed)).astype(BF16)
        side2[c] = spread_terms(1, c, lambda to: dot(w2_turned[to], hidden))

    def stage_cross2(c):
        far2[c] = cross(1, c, side2[c])

    def stage_last(c):
        far2[c].wait_recv()
        out_ref[:, span(c)] = (rfull[c, h].astype(F32) + gathered(1, c)).astype(BF16)

    stages = [
        stage_out,
        stage_cross1,
        stage_resid,
        stage_pass,
        stage_feed,
        stage_cross2,
        stage_last,
    ]
    for stage in stages:
        for c in range(chunks):
            stage(c)
    for copy in sent:
        copy.wait_send()


def local(
    tile_count,
    group_count,
    tiles,
    first_norm_gain,
    query_key_value_weight,
    attention_out_weight,
    second_norm_gain,
    first_feed_weight,
    second_feed_weight,
    slide_tile_counts,
    dilation_head_offsets,
):
    rows, share = tiles.shape
    heads = dilation_head_offsets.shape[0]
    levels = tile_count.bit_length() - 1
    chunks = rows // CHUNK
    _, key_rows = key_layout(rows, tile_count)
    select_rows = max(16, sum(padded_rows(rows, level) for level in range(1, levels)))
    copies = 10 * chunks + tile_count - 1
    vmem = pl.BlockSpec(memory_space=pltpu.VMEM)
    hbm = pl.BlockSpec(memory_space=pltpu.HBM)
    hidden = first_feed_weight.shape[1]
    width = share * group_count
    return pl.pallas_call(
        functools.partial(kernel, tile_count, group_count, slide_tile_counts.shape[0]),
        out_shape=jax.ShapeDtypeStruct((share, rows), BF16),
        in_specs=[hbm] * 9,
        out_specs=vmem,
        scratch_shapes=[
            pltpu.VMEM((share, rows), BF16),
            pltpu.VMEM((width,), F32),
            pltpu.VMEM((width,), F32),
            pltpu.VMEM((width, CHUNK), F32),
            pltpu.VMEM((width, CHUNK), F32),
            pltpu.SMEM(slide_tile_counts.shape, jnp.int32),
            pltpu.SMEM(dilation_head_offsets.shape, jnp.int32),
            pltpu.VMEM((3, share, width), BF16),
            pltpu.VMEM((share, width), BF16),
            pltpu.VMEM((width, hidden), BF16),
            pltpu.VMEM((hidden, width), BF16),
            pltpu.VMEM((group_count, share, share), BF16),
            pltpu.VMEM((hidden, width), BF16),
            pltpu.VMEM((group_count, share, hidden), BF16),
            pltpu.VMEM((chunks, group_count, share, CHUNK), BF16),
            pltpu.VMEM((chunks, group_count, share, CHUNK), BF16),
            pltpu.VMEM((heads, rows, WIDE), BF16),
            pltpu.VMEM((heads, key_rows, WIDE), BF16),
            pltpu.VMEM((heads, select_rows, WIDE), BF16),
            pltpu.VMEM((heads, rows, WIDE), F32),
            pltpu.VMEM((heads, rows, WIDE), F32),
            pltpu.VMEM((share, rows), BF16),
            pltpu.VMEM((2, chunks, 2, share, CHUNK), F32),
            pltpu.VMEM((2, chunks, 2, share, CHUNK), BF16),
            pltpu.VMEM((2, chunks, 2, share, CHUNK), BF16),
            pltpu.VMEM((2, chunks, share, CHUNK), BF16),
            pltpu.VMEM((2, chunks, share, CHUNK), BF16),
            pltpu.SemaphoreType.DMA((9,)),
            pltpu.SemaphoreType.DMA((copies,)),
            pltpu.SemaphoreType.DMA((copies,)),
        ],
        compiler_params=pltpu.CompilerParams(
            collective_id=0, has_side_effects=True, vmem_limit_bytes=64 << 20
        ),
    )(
        tiles.T,
        first_norm_gain,
        jnp.transpose(query_key_value_weight, (1, 2, 0)),
        attention_out_weight,
        second_norm_gain,
        first_feed_weight,
        second_feed_weight,
        slide_tile_counts,
        dilation_head_offsets,
    ).T


def solution(mesh):
    return jax.shard_map(
        functools.partial(local, mesh.shape["tile"], mesh.shape["head"]),
        mesh=mesh,
        in_specs=(
            P("tile", "head"),
            P(),
            P(None, None, "head"),
            P("head", None),
            P(),
            P(None, "head"),
            P("head", None),
            P(),
            P("head"),
        ),
        out_specs=P("tile", "head"),
        check_vma=False,
    )
```

```python
import functools

import jax
import jax.numpy as jnp
from jax import lax
from jax.experimental import pallas as pl
from jax.experimental.pallas import tpu as pltpu
from jax.sharding import PartitionSpec as P

HDIM = 64
WIDE = 2 * HDIM
CHUNK = 128
MASKED = -1e30
F32 = jnp.float32
BF16 = jnp.bfloat16


def dot(left, right):
    return jnp.dot(left, right, preferred_element_type=F32)


def padded_rows(rows, level):
    return -(-(rows >> level) // 16) * 16


def key_parts(rows, tile_count):
    levels = tile_count.bit_length() - 1
    return rows // CHUNK if (CHUNK >> (levels - 1)) % 16 == 0 else 1


def key_layout(rows, tile_count):
    pieces, start = {}, rows
    for m in range(1, tile_count):
        level = m.bit_length() - 1
        count = padded_rows(rows, level)
        pieces[m] = (level, start, count)
        start += count
    return pieces, start


def layer_norm_columns(values, gain):
    width = values.shape[0]
    center = jnp.sum(values, axis=0, keepdims=True) / width
    square = jnp.sum(values * values, axis=0, keepdims=True) / width
    scale = lax.rsqrt(square - center * center + 1e-05)
    return ((values - center) * scale * gain).astype(BF16)


def kernel(
    tile_count,
    group_count,
    slide_count,
    tiles_hbm,
    gain1_hbm,
    qkv_hbm,
    wo_hbm,
    gain2_hbm,
    w1_hbm,
    w2_hbm,
    counts_hbm,
    offsets_hbm,
    out_ref,
    tiles_ref,
    gain1_row,
    gain2_row,
    gain1,
    gain2,
    counts_ref,
    offsets_ref,
    wqkv,
    wo,
    w1,
    w2,
    wo_turned,
    w1_turned,
    w2_turned,
    xfull,
    rfull,
    qaug,
    kvbuf,
    select_buf,
    top_buf,
    acc_buf,
    attn_buf,
    keep_buf,
    side_send,
    side_recv,
    far_send,
    far_recv,
    load_sem,
    send_sem,
    recv_sem,
):
    share, rows = tiles_ref.shape
    heads = offsets_ref.shape[0]
    levels = tile_count.bit_length() - 1
    chunks = rows // CHUNK
    width = share * group_count
    pieces, key_rows = key_layout(rows, tile_count)
    t = lax.axis_index("tile")
    h = lax.axis_index("head")
    sib, far, diag = h ^ 1, h ^ 2, h ^ 3

    loads = [
        pltpu.make_async_copy(src, dst, load_sem.at[i])
        for i, (src, dst) in enumerate(
            (
                (tiles_hbm, tiles_ref),
                (counts_hbm, counts_ref),
                (offsets_hbm, offsets_ref),
                (gain1_hbm, gain1_row),
                (gain2_hbm, gain2_row),
                (wo_hbm, wo),
                (w1_hbm, w1),
                (w2_hbm, w2),
                (qkv_hbm, wqkv),
            )
        )
    ]
    for load in loads:
        load.start()

    barrier = pltpu.get_barrier_semaphore()
    for peer in (sib, far):
        pl.semaphore_signal(
            barrier, inc=1, device_id=(t, peer), device_id_type=pl.DeviceIdType.MESH
        )
    for m in range(1, tile_count):
        pl.semaphore_signal(
            barrier, inc=1, device_id=(t ^ m, h), device_id_type=pl.DeviceIdType.MESH
        )
    pl.semaphore_wait(barrier, tile_count + 1)

    used = [0]
    sent = []

    def send(src, dst, tile, head):
        index = used[0]
        used[0] += 1
        copy = pltpu.make_async_remote_copy(
            src_ref=src,
            dst_ref=dst,
            send_sem=send_sem.at[index],
            recv_sem=recv_sem.at[index],
            device_id=(tile, head),
            device_id_type=pl.DeviceIdType.MESH,
        )
        copy.start()
        sent.append(copy)
        return copy

    def span(c):
        return pl.ds(c * CHUNK, CHUNK)

    loads[0].wait()
    own_far, own_side = [], []
    for c in range(chunks):
        own_far.append(send(tiles_ref.at[:, span(c)], xfull.at[c, h], t, far))
    for c in range(chunks):
        own_side.append(send(tiles_ref.at[:, span(c)], xfull.at[c, h], t, sib))
    loads[1].wait()
    loads[2].wait()

    lane_row = lax.broadcasted_iota(jnp.int32, (1, WIDE), 1)
    low = jnp.full((1, WIDE), -1, jnp.int32)
    high = jnp.full((1, WIDE), 1 << 30, jnp.int32)
    total = jnp.int32(0)
    for j in range(slide_count - 1):
        total = total + counts_ref[j]
        high = jnp.where(lane_row == HDIM + j, total, high)
        low = jnp.where(lane_row == HDIM + j + 1, total, low)
    is_slide = (lane_row >= HDIM) & (lane_row < HDIM + slide_count)

    def row_iota(count):
        return lax.broadcasted_iota(jnp.int32, (count, WIDE), 0)

    def lane_iota(count):
        return lax.broadcasted_iota(jnp.int32, (count, WIDE), 1)

    offs = [offsets_ref[i] for i in range(heads)]

    def query_features(i):
        posn = t * rows + row_iota(rows)
        lane = lane_iota(rows)
        inside = (posn >= low) & (posn < high) & is_slide
        feats = jnp.where(inside, F32(1), F32(0))
        for level in range(1, levels):
            step = 1 << level
            other = (posn & (step - 1)) != (offs[i] & (step - 1))
            feats = jnp.where((lane == HDIM + slide_count + level - 1) & other, F32(1), feats)
        return feats

    for i in range(heads):
        qaug[i] = query_features(i).astype(BF16)

    for load in loads[3:]:
        load.wait()
    gain1[...] = jnp.broadcast_to(gain1_row[...][None], (CHUNK, width)).T
    gain2[...] = jnp.broadcast_to(gain2_row[...][None], (CHUNK, width)).T
    turned = wo[...].T
    for b in range(group_count):
        wo_turned[b] = turned[b * share : (b + 1) * share]
    w1_turned[...] = w1[...].T
    turned = w2[...].T
    for b in range(group_count):
        w2_turned[b] = turned[b * share : (b + 1) * share]

    def columns(blocks):
        return jnp.concatenate(blocks, axis=0).astype(F32)

    def project(c, passed):
        own_side[c].wait_recv()
        passed.wait_recv()
        own = tiles_ref[:, span(c)]
        blocks = [jnp.where(h == b, own, xfull[c, b]) for b in range(group_count)]
        normed = layer_norm_columns(columns(blocks), gain1[...])
        query, key, value = [dot(wqkv[kind], normed) for kind in range(3)]
        query = query.astype(BF16).astype(F32) * F32(HDIM ** (-0.5))
        for i in range(heads):
            own = slice(i * HDIM, (i + 1) * HDIM)
            features = jnp.concatenate([query[own], query[own]], axis=0).T
            first = lane_iota(CHUNK) < HDIM
            qaug[i, span(c), :] = jnp.where(
                first, features, qaug[i, span(c), :].astype(F32)
            ).astype(BF16)
            kvbuf[i, span(c), :] = jnp.concatenate([key[own], value[own]], axis=0).T.astype(BF16)

    passed = []
    for c in range(chunks):
        own_far[c].wait_recv()
        passed.append(send(xfull.at[c, far], xfull.at[c, far], t, sib))
    parts = key_parts(rows, tile_count)
    key_copy = {}
    select_start, at = {}, 0
    for level in range(1, levels):
        select_start[level] = at
        at += padded_rows(rows, level)

    def send_keys(part):
        span_rows = rows // parts
        source = pl.ds(part * span_rows, span_rows)
        for level in [0] + list(range(levels - 1, 0, -1)):
            count = padded_rows(rows, level) // parts
            if level == 0:
                src = kvbuf.at[:, source]
            else:
                step = 1 << level
                place = pl.ds(select_start[level] + part * count, count)
                want = lax.broadcasted_iota(jnp.int32, (count, span_rows), 0) * step
                have = lax.broadcasted_iota(jnp.int32, (count, span_rows), 1)
                for i in range(heads):
                    pick = jnp.where(have == want + (offs[i] & (step - 1)), F32(1), F32(0))
                    select_buf[i, place, :] = dot(
                        pick.astype(BF16), kvbuf[i, source, :]
                    ).astype(BF16)
                src = select_buf.at[:, place]
            for m in range(1 << level, 2 << level):
                start = pieces[m][1] + part * count
                key_copy[m, part] = send(src, kvbuf.at[:, pl.ds(start, count)], t ^ m, h)

    for c in range(chunks):
        project(c, passed[c])
        if parts == chunks:
            send_keys(c)
    if parts != chunks:
        send_keys(0)

    def prepare(i, members, level):
        off = offs[i]
        step = 1 << level
        augs, posns, keys = [], [], []
        for m in members:
            if m == 0:
                start, count = 0, rows
            else:
                _, start, count = pieces[m]
            local = row_iota(count) * step + (off & (step - 1))
            posn = (t ^ m) * rows + local
            both = kvbuf[i, pl.ds(start, count), :].astype(F32)
            inside = (posn >= low) & (posn < high) & (local < rows)
            feats = jnp.where(is_slide & jnp.logical_not(inside), F32(MASKED), F32(0))
            if level > 0:
                feats = jnp.where(
                    lane_iota(count) == HDIM + slide_count + level - 1, F32(MASKED), feats
                )
            augs.append(jnp.where(lane_iota(count) < HDIM, both, feats).astype(BF16))
            keys.append(both)
            posns.append(posn)
        aug = augs[0] if len(augs) == 1 else jnp.concatenate(augs, axis=0)
        both = keys[0] if len(keys) == 1 else jnp.concatenate(keys, axis=0)
        posn = posns[0] if len(posns) == 1 else jnp.concatenate(posns, axis=0)
        summed = jnp.where(lane_iota(both.shape[0]) < HDIM, F32(1), both)
        weights = []
        for l in range(level, levels):
            mod = (1 << l) - 1
            chosen = summed
            if l > level:
                chosen = jnp.where((posn & mod) == (off & mod), summed, F32(0))
            weights.append(chosen.astype(BF16))
        return aug, weights

    def attend(i, prepared, level, first, begin, count):
        aug, weights = prepared
        query = pl.ds(begin, count)
        scores = lax.dot_general(
            qaug[i, query, :], aug, (((1,), (1,)), ((), ())), preferred_element_type=F32
        )
        top = jnp.max(scores, axis=1, keepdims=True)
        if not first:
            before = top_buf[i, query, 0:1]
            top = jnp.maximum(top, before)
        expo = jnp.exp(scores - top).astype(BF16)
        acc = None
        query_posn = t * rows + begin + row_iota(count)
        for l in range(level, levels):
            mod = (1 << l) - 1
            term = dot(expo, weights[l - level])
            if l > 0:
                term = jnp.where((query_posn & mod) == (offs[i] & mod), term, F32(0))
            acc = term if acc is None else acc + term
        if not first:
            acc = acc + acc_buf[i, query, :] * jnp.exp(before - top)
        acc_buf[i, query, :] = acc
        top_buf[i, query, :] = jnp.broadcast_to(top, (count, WIDE))

    def arrived(level):
        members = list(range(1 << level, 2 << level))
        for m in members:
            for part in range(parts):
                key_copy[m, part].wait_recv()
        return members

    for i in range(heads):
        attend(i, prepare(i, [0], 0), 0, True, 0, rows)
    for level in range(levels - 1):
        members = arrived(level)
        for i in range(heads):
            attend(i, prepare(i, members, level), level, False, 0, rows)
    members = arrived(levels - 1)
    last_keys = [prepare(i, members, levels - 1) for i in range(heads)]

    def finish(c):
        for i in range(heads):
            attend(i, last_keys[i], levels - 1, False, c * CHUNK, CHUNK)
            acc = acc_buf[i, span(c), :].T
            attn_buf[i * HDIM : (i + 1) * HDIM, span(c)] = (acc[HDIM:WIDE] / acc[0:1]).astype(BF16)

    side1, far1, side2, far2 = {}, {}, {}, {}
    res_far, res_side, res_pass = {}, {}, {}

    def spread_terms(which, c, block):
        for j, to in enumerate((sib, diag)):
            side_send[which, c, j] = block(to).astype(BF16)
        copy = send(side_send.at[which, c], side_recv.at[which, c], t, sib)
        for j, to in enumerate((far, h)):
            keep_buf[which, c, j] = block(to)
        return copy

    def cross(which, c, side):
        side.wait_recv()
        far_send[which, c] = (
            keep_buf[which, c, 0].astype(BF16).astype(F32) + side_recv[which, c, 1].astype(F32)
        ).astype(BF16)
        return send(far_send.at[which, c], far_recv.at[which, c], t, far)

    def gathered(which, c):
        return (
            keep_buf[which, c, 1].astype(BF16).astype(F32)
            + side_recv[which, c, 0].astype(F32)
            + far_recv[which, c].astype(F32)
        )

    def stage_out(c):
        finish(c)
        attn = attn_buf[:, span(c)]
        side1[c] = spread_terms(0, c, lambda to: dot(wo_turned[to], attn))

    def stage_cross1(c):
        far1[c] = cross(0, c, side1[c])

    def stage_resid(c):
        far1[c].wait_recv()
        rfull[c, h] = (tiles_ref[:, span(c)].astype(F32) + gathered(0, c)).astype(BF16)
        res_far[c] = send(rfull.at[c, h], rfull.at[c, h], t, far)
        res_side[c] = send(rfull.at[c, h], rfull.at[c, h], t, sib)

    def stage_pass(c):
        res_far[c].wait_recv()
        res_pass[c] = send(rfull.at[c, far], rfull.at[c, far], t, sib)

    def stage_feed(c):
        res_side[c].wait_recv()
        res_pass[c].wait_recv()
        blocks = [rfull[c, b] for b in range(group_count)]
        normed = layer_norm_columns(columns(blocks), gain2[...])
        hidden = jax.nn.gelu(dot(w1_turned[...], normed)).astype(BF16)
        side2[c] = spread_terms(1, c, lambda to: dot(w2_turned[to], hidden))

    def stage_cross2(c):
        far2[c] = cross(1, c, side2[c])

    def stage_last(c):
        far2[c].wait_recv()
        out_ref[:, span(c)] = (rfull[c, h].astype(F32) + gathered(1, c)).astype(BF16)

    def staged(ahead, behind):
        for c in range(chunks + 1):
            if c < chunks:
                ahead(c)
            if c > 0:
                behind(c - 1)

    staged(stage_out, stage_cross1)
    for stage in (stage_resid, stage_pass):
        for c in range(chunks):
            stage(c)
    staged(stage_feed, stage_cross2)
    for c in range(chunks):
        stage_last(c)
    for copy in sent:
        copy.wait_send()


def local(
    tile_count,
    group_count,
    tiles,
    first_norm_gain,
    query_key_value_weight,
    attention_out_weight,
    second_norm_gain,
    first_feed_weight,
    second_feed_weight,
    slide_tile_counts,
    dilation_head_offsets,
):
    rows, share = tiles.shape
    heads = dilation_head_offsets.shape[0]
    levels = tile_count.bit_length() - 1
    chunks = rows // CHUNK
    _, key_rows = key_layout(rows, tile_count)
    select_rows = max(16, sum(padded_rows(rows, level) for level in range(1, levels)))
    copies = 10 * chunks + (tile_count - 1) * key_parts(rows, tile_count)
    vmem = pl.BlockSpec(memory_space=pltpu.VMEM)
    hbm = pl.BlockSpec(memory_space=pltpu.HBM)
    hidden = first_feed_weight.shape[1]
    width = share * group_count
    return pl.pallas_call(
        functools.partial(kernel, tile_count, group_count, slide_tile_counts.shape[0]),
        out_shape=jax.ShapeDtypeStruct((share, rows), BF16),
        in_specs=[hbm] * 9,
        out_specs=vmem,
        scratch_shapes=[
            pltpu.VMEM((share, rows), BF16),
            pltpu.VMEM((width,), F32),
            pltpu.VMEM((width,), F32),
            pltpu.VMEM((width, CHUNK), F32),
            pltpu.VMEM((width, CHUNK), F32),
            pltpu.SMEM(slide_tile_counts.shape, jnp.int32),
            pltpu.SMEM(dilation_head_offsets.shape, jnp.int32),
            pltpu.VMEM((3, share, width), BF16),
            pltpu.VMEM((share, width), BF16),
            pltpu.VMEM((width, hidden), BF16),
            pltpu.VMEM((hidden, width), BF16),
            pltpu.VMEM((group_count, share, share), BF16),
            pltpu.VMEM((hidden, width), BF16),
            pltpu.VMEM((group_count, share, hidden), BF16),
            pltpu.VMEM((chunks, group_count, share, CHUNK), BF16),
            pltpu.VMEM((chunks, group_count, share, CHUNK), BF16),
            pltpu.VMEM((heads, rows, WIDE), BF16),
            pltpu.VMEM((heads, key_rows, WIDE), BF16),
            pltpu.VMEM((heads, select_rows, WIDE), BF16),
            pltpu.VMEM((heads, rows, WIDE), F32),
            pltpu.VMEM((heads, rows, WIDE), F32),
            pltpu.VMEM((share, rows), BF16),
            pltpu.VMEM((2, chunks, 2, share, CHUNK), F32),
            pltpu.VMEM((2, chunks, 2, share, CHUNK), BF16),
            pltpu.VMEM((2, chunks, 2, share, CHUNK), BF16),
            pltpu.VMEM((2, chunks, share, CHUNK), BF16),
            pltpu.VMEM((2, chunks, share, CHUNK), BF16),
            pltpu.SemaphoreType.DMA((9,)),
            pltpu.SemaphoreType.DMA((copies,)),
            pltpu.SemaphoreType.DMA((copies,)),
        ],
        compiler_params=pltpu.CompilerParams(
            collective_id=0, has_side_effects=True, vmem_limit_bytes=64 << 20
        ),
    )(
        tiles.T,
        first_norm_gain,
        jnp.transpose(query_key_value_weight, (1, 2, 0)),
        attention_out_weight,
        second_norm_gain,
        first_feed_weight,
        second_feed_weight,
        slide_tile_counts,
        dilation_head_offsets,
    ).T


def solution(mesh):
    return jax.shard_map(
        functools.partial(local, mesh.shape["tile"], mesh.shape["head"]),
        mesh=mesh,
        in_specs=(
            P("tile", "head"),
            P(),
            P(None, None, "head"),
            P("head", None),
            P(),
            P(None, "head"),
            P("head", None),
            P(),
            P("head"),
        ),
        out_specs=P("tile", "head"),
        check_vma=False,
    )
```

```python
import functools

import jax
import jax.numpy as jnp
from jax import lax
from jax.experimental import pallas as pl
from jax.experimental.pallas import tpu as pltpu
from jax.sharding import PartitionSpec as P

HDIM = 64
WIDE = 2 * HDIM
CHUNK = 128
MASKED = -1e30
F32 = jnp.float32
BF16 = jnp.bfloat16


def dot(left, right):
    return jnp.dot(left, right, preferred_element_type=F32)


def padded_rows(rows, level):
    return -(-(rows >> level) // 16) * 16


def key_parts(rows, tile_count):
    levels = tile_count.bit_length() - 1
    return rows // CHUNK if (CHUNK >> (levels - 1)) % 16 == 0 else 1


def key_layout(rows, tile_count):
    pieces, start = {}, rows
    for m in range(1, tile_count):
        level = m.bit_length() - 1
        count = padded_rows(rows, level)
        pieces[m] = (level, start, count)
        start += count
    return pieces, start


def layer_norm_columns(values, gain):
    width = values.shape[0]
    center = jnp.sum(values, axis=0, keepdims=True) / width
    square = jnp.sum(values * values, axis=0, keepdims=True) / width
    scale = lax.rsqrt(square - center * center + 1e-05)
    return ((values - center) * scale * gain).astype(BF16)


def kernel(
    tile_count,
    group_count,
    slide_count,
    tiles_hbm,
    gain1_hbm,
    qkv_hbm,
    wo_hbm,
    gain2_hbm,
    w1_hbm,
    w2_hbm,
    counts_hbm,
    offsets_hbm,
    out_ref,
    tiles_ref,
    gain1_row,
    gain2_row,
    gain1,
    gain2,
    counts_ref,
    offsets_ref,
    wqkv,
    wo,
    w1,
    w2,
    wo_turned,
    w1_turned,
    w2_turned,
    xfull,
    rfull,
    qaug,
    kvbuf,
    select_buf,
    top_buf,
    acc_buf,
    attn_buf,
    keep_buf,
    side_send,
    side_recv,
    far_send,
    far_recv,
    load_sem,
    send_sem,
    recv_sem,
):
    share, rows = tiles_ref.shape
    heads = offsets_ref.shape[0]
    levels = tile_count.bit_length() - 1
    chunks = rows // CHUNK
    width = share * group_count
    pieces, key_rows = key_layout(rows, tile_count)
    t = lax.axis_index("tile")
    h = lax.axis_index("head")
    sib, far, diag = h ^ 1, h ^ 2, h ^ 3

    loads = [
        pltpu.make_async_copy(src, dst, load_sem.at[i])
        for i, (src, dst) in enumerate(
            (
                (tiles_hbm, tiles_ref),
                (counts_hbm, counts_ref),
                (offsets_hbm, offsets_ref),
                (gain1_hbm, gain1_row),
                (gain2_hbm, gain2_row),
                (wo_hbm, wo),
                (w1_hbm, w1),
                (w2_hbm, w2),
                (qkv_hbm, wqkv),
            )
        )
    ]
    for load in loads:
        load.start()

    barrier = pltpu.get_barrier_semaphore()
    for peer in (sib, far):
        pl.semaphore_signal(
            barrier, inc=1, device_id=(t, peer), device_id_type=pl.DeviceIdType.MESH
        )
    for m in range(1, tile_count):
        pl.semaphore_signal(
            barrier, inc=1, device_id=(t ^ m, h), device_id_type=pl.DeviceIdType.MESH
        )
    pl.semaphore_wait(barrier, tile_count + 1)

    used = [0]
    sent = []

    def send(src, dst, tile, head):
        index = used[0]
        used[0] += 1
        copy = pltpu.make_async_remote_copy(
            src_ref=src,
            dst_ref=dst,
            send_sem=send_sem.at[index],
            recv_sem=recv_sem.at[index],
            device_id=(tile, head),
            device_id_type=pl.DeviceIdType.MESH,
        )
        copy.start()
        sent.append(copy)
        return copy

    def span(c):
        return pl.ds(c * CHUNK, CHUNK)

    loads[0].wait()
    own_far, own_side = [], []
    for c in range(chunks):
        own_far.append(send(tiles_ref.at[:, span(c)], xfull.at[c, h], t, far))
    for c in range(chunks):
        own_side.append(send(tiles_ref.at[:, span(c)], xfull.at[c, h], t, sib))
    loads[1].wait()
    loads[2].wait()

    lane_row = lax.broadcasted_iota(jnp.int32, (1, WIDE), 1)
    low = jnp.full((1, WIDE), -1, jnp.int32)
    high = jnp.full((1, WIDE), 1 << 30, jnp.int32)
    total = jnp.int32(0)
    for j in range(slide_count - 1):
        total = total + counts_ref[j]
        high = jnp.where(lane_row == HDIM + j, total, high)
        low = jnp.where(lane_row == HDIM + j + 1, total, low)
    is_slide = (lane_row >= HDIM) & (lane_row < HDIM + slide_count)

    def row_iota(count):
        return lax.broadcasted_iota(jnp.int32, (count, WIDE), 0)

    def lane_iota(count):
        return lax.broadcasted_iota(jnp.int32, (count, WIDE), 1)

    offs = [offsets_ref[i] for i in range(heads)]

    def query_features(i):
        posn = t * rows + row_iota(rows)
        lane = lane_iota(rows)
        inside = (posn >= low) & (posn < high) & is_slide
        feats = jnp.where(inside, F32(1), F32(0))
        for level in range(1, levels):
            step = 1 << level
            other = (posn & (step - 1)) != (offs[i] & (step - 1))
            feats = jnp.where((lane == HDIM + slide_count + level - 1) & other, F32(1), feats)
        return feats

    for i in range(heads):
        qaug[i] = query_features(i).astype(BF16)

    for load in loads[3:]:
        load.wait()
    gain1[...] = jnp.broadcast_to(gain1_row[...][None], (CHUNK, width)).T
    gain2[...] = jnp.broadcast_to(gain2_row[...][None], (CHUNK, width)).T
    turned = wo[...].T
    for b in range(group_count):
        wo_turned[b] = turned[b * share : (b + 1) * share]
    w1_turned[...] = w1[...].T
    turned = w2[...].T
    for b in range(group_count):
        w2_turned[b] = turned[b * share : (b + 1) * share]

    def columns(blocks):
        return jnp.concatenate(blocks, axis=0).astype(F32)

    def project(c, passed):
        own_side[c].wait_recv()
        passed.wait_recv()
        own = tiles_ref[:, span(c)]
        blocks = [jnp.where(h == b, own, xfull[c, b]) for b in range(group_count)]
        normed = layer_norm_columns(columns(blocks), gain1[...])
        query, key, value = [dot(wqkv[kind], normed) for kind in range(3)]
        query = query.astype(BF16).astype(F32) * F32(HDIM ** (-0.5))
        for i in range(heads):
            own = slice(i * HDIM, (i + 1) * HDIM)
            features = jnp.concatenate([query[own], query[own]], axis=0).T
            first = lane_iota(CHUNK) < HDIM
            qaug[i, span(c), :] = jnp.where(
                first, features, qaug[i, span(c), :].astype(F32)
            ).astype(BF16)
            kvbuf[i, span(c), :] = jnp.concatenate([key[own], value[own]], axis=0).T.astype(BF16)

    passed = []
    for c in range(chunks):
        own_far[c].wait_recv()
        passed.append(send(xfull.at[c, far], xfull.at[c, far], t, sib))
    parts = key_parts(rows, tile_count)
    key_copy = {}
    select_start, at = {}, 0
    for level in range(1, levels):
        select_start[level] = at
        at += padded_rows(rows, level)

    def send_keys(part):
        span_rows = rows // parts
        source = pl.ds(part * span_rows, span_rows)
        for level in range(levels - 1, -1, -1):
            count = padded_rows(rows, level) // parts
            if level == 0:
                src = kvbuf.at[:, source]
            else:
                step = 1 << level
                place = pl.ds(select_start[level] + part * count, count)
                want = lax.broadcasted_iota(jnp.int32, (count, span_rows), 0) * step
                have = lax.broadcasted_iota(jnp.int32, (count, span_rows), 1)
                for i in range(heads):
                    pick = jnp.where(have == want + (offs[i] & (step - 1)), F32(1), F32(0))
                    select_buf[i, place, :] = dot(
                        pick.astype(BF16), kvbuf[i, source, :]
                    ).astype(BF16)
                src = select_buf.at[:, place]
            for m in range(1 << level, 2 << level):
                start = pieces[m][1] + part * count
                key_copy[m, part] = send(src, kvbuf.at[:, pl.ds(start, count)], t ^ m, h)

    for c in range(chunks):
        project(c, passed[c])
        if parts == chunks:
            send_keys(c)
    if parts != chunks:
        send_keys(0)

    def prepare(i, members, level):
        off = offs[i]
        step = 1 << level
        augs, posns, keys = [], [], []
        for m in members:
            if m == 0:
                start, count = 0, rows
            else:
                _, start, count = pieces[m]
            local = row_iota(count) * step + (off & (step - 1))
            posn = (t ^ m) * rows + local
            both = kvbuf[i, pl.ds(start, count), :].astype(F32)
            inside = (posn >= low) & (posn < high) & (local < rows)
            feats = jnp.where(is_slide & jnp.logical_not(inside), F32(MASKED), F32(0))
            if level > 0:
                feats = jnp.where(
                    lane_iota(count) == HDIM + slide_count + level - 1, F32(MASKED), feats
                )
            augs.append(jnp.where(lane_iota(count) < HDIM, both, feats).astype(BF16))
            keys.append(both)
            posns.append(posn)
        aug = augs[0] if len(augs) == 1 else jnp.concatenate(augs, axis=0)
        both = keys[0] if len(keys) == 1 else jnp.concatenate(keys, axis=0)
        posn = posns[0] if len(posns) == 1 else jnp.concatenate(posns, axis=0)
        summed = jnp.where(lane_iota(both.shape[0]) < HDIM, F32(1), both)
        weights = []
        for l in range(level, levels):
            mod = (1 << l) - 1
            chosen = summed
            if l > level:
                chosen = jnp.where((posn & mod) == (off & mod), summed, F32(0))
            weights.append(chosen.astype(BF16))
        return aug, weights

    def attend(i, prepared, level, first, begin, count):
        aug, weights = prepared
        query = pl.ds(begin, count)
        scores = lax.dot_general(
            qaug[i, query, :], aug, (((1,), (1,)), ((), ())), preferred_element_type=F32
        )
        top = jnp.max(scores, axis=1, keepdims=True)
        if not first:
            before = top_buf[i, query, 0:1]
            top = jnp.maximum(top, before)
        expo = jnp.exp(scores - top).astype(BF16)
        acc = None
        query_posn = t * rows + begin + row_iota(count)
        for l in range(level, levels):
            mod = (1 << l) - 1
            term = dot(expo, weights[l - level])
            if l > 0:
                term = jnp.where((query_posn & mod) == (offs[i] & mod), term, F32(0))
            acc = term if acc is None else acc + term
        if not first:
            acc = acc + acc_buf[i, query, :] * jnp.exp(before - top)
        acc_buf[i, query, :] = acc
        top_buf[i, query, :] = jnp.broadcast_to(top, (count, WIDE))

    def arrived(level):
        members = list(range(1 << level, 2 << level))
        for m in members:
            for part in range(parts):
                key_copy[m, part].wait_recv()
        return members

    for i in range(heads):
        attend(i, prepare(i, [0], 0), 0, True, 0, rows)
    for level in range(levels - 1):
        members = arrived(level)
        for i in range(heads):
            attend(i, prepare(i, members, level), level, False, 0, rows)
    members = arrived(levels - 1)
    last_keys = [prepare(i, members, levels - 1) for i in range(heads)]

    def finish(c):
        for i in range(heads):
            attend(i, last_keys[i], levels - 1, False, c * CHUNK, CHUNK)
            acc = acc_buf[i, span(c), :].T
            attn_buf[i * HDIM : (i + 1) * HDIM, span(c)] = (acc[HDIM:WIDE] / acc[0:1]).astype(BF16)

    side1, far1, side2, far2 = {}, {}, {}, {}
    res_far, res_side, res_pass = {}, {}, {}

    def spread_terms(which, c, block):
        for j, to in enumerate((sib, diag)):
            side_send[which, c, j] = block(to).astype(BF16)
        copy = send(side_send.at[which, c], side_recv.at[which, c], t, sib)
        for j, to in enumerate((far, h)):
            keep_buf[which, c, j] = block(to)
        return copy

    def cross(which, c, side):
        side.wait_recv()
        far_send[which, c] = (
            keep_buf[which, c, 0].astype(BF16).astype(F32) + side_recv[which, c, 1].astype(F32)
        ).astype(BF16)
        return send(far_send.at[which, c], far_recv.at[which, c], t, far)

    def gathered(which, c):
        return (
            keep_buf[which, c, 1].astype(BF16).astype(F32)
            + side_recv[which, c, 0].astype(F32)
            + far_recv[which, c].astype(F32)
        )

    def stage_out(c):
        finish(c)
        attn = attn_buf[:, span(c)]
        side1[c] = spread_terms(0, c, lambda to: dot(wo_turned[to], attn))

    def stage_cross1(c):
        far1[c] = cross(0, c, side1[c])

    def stage_resid(c):
        far1[c].wait_recv()
        rfull[c, h] = (tiles_ref[:, span(c)].astype(F32) + gathered(0, c)).astype(BF16)
        res_far[c] = send(rfull.at[c, h], rfull.at[c, h], t, far)
        res_side[c] = send(rfull.at[c, h], rfull.at[c, h], t, sib)

    def stage_pass(c):
        res_far[c].wait_recv()
        res_pass[c] = send(rfull.at[c, far], rfull.at[c, far], t, sib)

    def stage_feed(c):
        res_side[c].wait_recv()
        res_pass[c].wait_recv()
        blocks = [rfull[c, b] for b in range(group_count)]
        normed = layer_norm_columns(columns(blocks), gain2[...])
        hidden = jax.nn.gelu(dot(w1_turned[...], normed)).astype(BF16)
        side2[c] = spread_terms(1, c, lambda to: dot(w2_turned[to], hidden))

    def stage_cross2(c):
        far2[c] = cross(1, c, side2[c])

    def stage_last(c):
        far2[c].wait_recv()
        out_ref[:, span(c)] = (rfull[c, h].astype(F32) + gathered(1, c)).astype(BF16)

    def staged(ahead, behind):
        for c in range(chunks + 1):
            if c < chunks:
                ahead(c)
            if c > 0:
                behind(c - 1)

    staged(stage_out, stage_cross1)
    for stage in (stage_resid, stage_pass):
        for c in range(chunks):
            stage(c)
    staged(stage_feed, stage_cross2)
    for c in range(chunks):
        stage_last(c)
    for copy in sent:
        copy.wait_send()


def local(
    tile_count,
    group_count,
    tiles,
    first_norm_gain,
    query_key_value_weight,
    attention_out_weight,
    second_norm_gain,
    first_feed_weight,
    second_feed_weight,
    slide_tile_counts,
    dilation_head_offsets,
):
    rows, share = tiles.shape
    heads = dilation_head_offsets.shape[0]
    levels = tile_count.bit_length() - 1
    chunks = rows // CHUNK
    _, key_rows = key_layout(rows, tile_count)
    select_rows = max(16, sum(padded_rows(rows, level) for level in range(1, levels)))
    copies = 10 * chunks + (tile_count - 1) * key_parts(rows, tile_count)
    vmem = pl.BlockSpec(memory_space=pltpu.VMEM)
    hbm = pl.BlockSpec(memory_space=pltpu.HBM)
    hidden = first_feed_weight.shape[1]
    width = share * group_count
    return pl.pallas_call(
        functools.partial(kernel, tile_count, group_count, slide_tile_counts.shape[0]),
        out_shape=jax.ShapeDtypeStruct((share, rows), BF16),
        in_specs=[hbm] * 9,
        out_specs=vmem,
        scratch_shapes=[
            pltpu.VMEM((share, rows), BF16),
            pltpu.VMEM((width,), F32),
            pltpu.VMEM((width,), F32),
            pltpu.VMEM((width, CHUNK), F32),
            pltpu.VMEM((width, CHUNK), F32),
            pltpu.SMEM(slide_tile_counts.shape, jnp.int32),
            pltpu.SMEM(dilation_head_offsets.shape, jnp.int32),
            pltpu.VMEM((3, share, width), BF16),
            pltpu.VMEM((share, width), BF16),
            pltpu.VMEM((width, hidden), BF16),
            pltpu.VMEM((hidden, width), BF16),
            pltpu.VMEM((group_count, share, share), BF16),
            pltpu.VMEM((hidden, width), BF16),
            pltpu.VMEM((group_count, share, hidden), BF16),
            pltpu.VMEM((chunks, group_count, share, CHUNK), BF16),
            pltpu.VMEM((chunks, group_count, share, CHUNK), BF16),
            pltpu.VMEM((heads, rows, WIDE), BF16),
            pltpu.VMEM((heads, key_rows, WIDE), BF16),
            pltpu.VMEM((heads, select_rows, WIDE), BF16),
            pltpu.VMEM((heads, rows, WIDE), F32),
            pltpu.VMEM((heads, rows, WIDE), F32),
            pltpu.VMEM((share, rows), BF16),
            pltpu.VMEM((2, chunks, 2, share, CHUNK), F32),
            pltpu.VMEM((2, chunks, 2, share, CHUNK), BF16),
            pltpu.VMEM((2, chunks, 2, share, CHUNK), BF16),
            pltpu.VMEM((2, chunks, share, CHUNK), BF16),
            pltpu.VMEM((2, chunks, share, CHUNK), BF16),
            pltpu.SemaphoreType.DMA((9,)),
            pltpu.SemaphoreType.DMA((copies,)),
            pltpu.SemaphoreType.DMA((copies,)),
        ],
        compiler_params=pltpu.CompilerParams(
            collective_id=0, has_side_effects=True, vmem_limit_bytes=64 << 20
        ),
    )(
        tiles.T,
        first_norm_gain,
        jnp.transpose(query_key_value_weight, (1, 2, 0)),
        attention_out_weight,
        second_norm_gain,
        first_feed_weight,
        second_feed_weight,
        slide_tile_counts,
        dilation_head_offsets,
    ).T


def solution(mesh):
    return jax.shard_map(
        functools.partial(local, mesh.shape["tile"], mesh.shape["head"]),
        mesh=mesh,
        in_specs=(
            P("tile", "head"),
            P(),
            P(None, None, "head"),
            P("head", None),
            P(),
            P(None, "head"),
            P("head", None),
            P(),
            P("head"),
        ),
        out_specs=P("tile", "head"),
        check_vma=False,
    )
```
